256 devices in a mesh: branch: 2 (over core), ctx: 16 (over y, z_hi), fsdp: 8 (over z_lo, x).
Axes of the slice: x: 4, y: 4, z: 8 (z_hi: 4, z_lo: 2; z = z_hi * 2 + z_lo), core: 2. Of those that a mesh axis runs over, the one named last changes fastest.
Arguments:
- hidden: bfloat16 [2, 6144, 6144], P('branch', 'ctx'), may hold values from -25 to 25
- stream: bfloat16 [2, 6144, 6144], P('branch', 'ctx', 'fsdp'), may hold values from -8 to 8
- w_query: bfloat16 [6144, 3072], P('ctx', 'fsdp'), may hold values from -0.078125 to 0.078125
- w_key: bfloat16 [6144, 3072], P('ctx', 'fsdp'), may hold values from -0.078125 to 0.078125
- w_value: bfloat16 [6144, 3072], P('ctx', 'fsdp'), may hold values from -0.078125 to 0.078125
- w_out: bfloat16 [3072, 6144], P('fsdp', 'ctx'), may hold values from -0.15625 to 0.15625
- out_gain: float32 [6144], P('fsdp'), may hold values from 0.1 to 1.9
- w_final: float32 [6144, 64], P('fsdp'), may hold values from -0.078125 to 0.078125
- latents: float32 [2, 6144, 64], P('branch', 'ctx'), may hold values from -1.5 to 1.5
- noise: float32 [2, 6144, 64], P('branch', 'ctx'), may hold values from -16 to 16
- timestep: int32 [1], replicated, may hold values from 20 to 979
Outputs:
- eps_pred: float32 [2, 6144, 64], P('branch', 'ctx')
- stepped: float32 [2, 6144, 64], P('branch', 'ctx')
The draws below stay inside these ranges and needn't reach their ends.
All inputs are finite; a program needn't handle non-finite values.
Results may differ from the reference program's by a relative error of at most 0.019.
Values may be sent and summed in bfloat16 or wider, within the bound.
No kernel may reach another device: no remote copies, remote signals or barrier semaphores. Data moves between devices by JAX's collectives and lax.ppermute only.
A program may use at most 128 MiB of HBM per device.

```python
import jax
import jax.numpy as jnp
from jax import lax

D = 6144
HEADS = 24
HEAD = 128
CHANNELS = 64
STEPS = 1000
TOKENS = 6144
N_FSDP = 8


def draw_hidden(key, part):
    key = jax.random.fold_in(key, 11)
    first = jax.random.fold_in(key, 0)
    values = jnp.clip(jax.random.normal(first, (2, TOKENS, D), jnp.float32), -5.0, 5.0)
    return values.astype(jnp.bfloat16)


def draw_stream(key, part):
    key = jax.random.fold_in(key, 23)
    first = jax.random.fold_in(key, 0)
    column = jnp.arange(D, dtype=jnp.float32) / D
    values = jnp.clip(jax.random.normal(first, (2, TOKENS, D), jnp.float32), -4.0, 4.0)
    values = values * 0.012 * jnp.power(3.0, column)
    return values.astype(jnp.bfloat16)


def spiked(entries, own_key, source, target, parts, factor):
    owner, partner = [(jnp.arange(entries.shape[dim]) // (entries.shape[dim] // parts)).reshape([-1 if axis == dim else 1 for axis in range(entries.ndim)]) for dim in (source, target)]
    chosen = jax.random.permutation(own_key, parts)[partner]
    strong = (owner == chosen) | (owner == (partner + parts // 2) % parts)
    return jnp.where(strong, factor * entries, entries)


def block_scale(rng, extent, shards, smallest, high):
    gain, own = 1.0, jax.random.fold_in(rng, 6)
    for position, blocks in shards:
        steps = jnp.exp(jax.random.uniform(jax.random.fold_in(own, position), (blocks,), jnp.float32, smallest / len(shards), high / len(shards)))
        gain = gain * jnp.repeat(steps, extent[position] // blocks).reshape([-1 if axis == position else 1 for axis in range(len(extent))])
    return gain


def bell_draw(rng, dims, width, bound, cuts=(), held_as=jnp.bfloat16):
    factor_of = block_scale(rng, dims, cuts, -0.22, 0.18) if cuts else 1.0
    result = jax.random.normal(rng, dims, jnp.float32) * width * factor_of
    return jnp.minimum(jnp.maximum(result, -bound), bound).astype(held_as)


def noise_with(stream_key, extent, scale, bound, pieces, heavy, kind=jnp.bfloat16):
    drawn = scale * jax.random.normal(stream_key, extent, jnp.float32)
    if pieces:
        drawn = drawn * block_scale(stream_key, extent, pieces, -0.22, 0.18)
    return jnp.clip(spiked(drawn, jax.random.fold_in(stream_key, 3), *heavy), -bound, bound).astype(kind)


def setup_inputs(seed: int = 0) -> dict:
    keys = jax.random.split(jax.random.key(seed), 12)
    return {
        "hidden": draw_hidden(jax.random.fold_in(keys[11], 71), 0),
        "stream": draw_stream(jax.random.fold_in(keys[11], 71), 0),
        "w_query": bell_draw(keys[2], (D, HEADS * HEAD), D ** -0.5, 0.078125, ((0, 16), (1, 8))),
        "w_key": bell_draw(keys[3], (D, HEADS * HEAD), D ** -0.5, 0.078125, ((0, 16), (1, 8))),
        "w_value": bell_draw(keys[4], (D, HEADS * HEAD), D ** -0.5, 0.078125, ((0, 16), (1, 8))),
        "w_out": noise_with(keys[5], (HEADS * HEAD, D), (HEADS * HEAD) ** -0.5, 0.15625, ((0, 8), (1, 16)), (0, 1, 16, 2.0)),
        "out_gain": jnp.clip(1.0 + 0.18 * jax.random.normal(keys[6], (D,), jnp.float32), 0.1, 1.9),
        "w_final": bell_draw(keys[7], (D, CHANNELS), D ** -0.5, 0.078125, ((0, 8),), jnp.float32),
        "latents": bell_draw(keys[8], (2, TOKENS, CHANNELS), 0.25, 1.5, ((0, 2), (1, 16)), jnp.float32),
        "noise": bell_draw(keys[9], (2, TOKENS, CHANNELS), 4.0, 16.0, ((0, 2), (1, 16)), jnp.float32),
        "timestep": jax.random.randint(keys[10], (1,), 20, 980).astype(jnp.int32),
    }


def plan(timestep):
    step_index = jnp.arange(STEPS, dtype=jnp.int32)
    betas = 0.0001 + (0.02 - 0.0001) * step_index.astype(jnp.float32) / (STEPS - 1)
    log_keep = jnp.cumsum(jnp.log1p(-betas))
    picked = (step_index == timestep[0]).astype(jnp.float32)
    beta_t = jnp.sum(picked * betas)
    abar_t = jnp.exp(jnp.sum(picked * log_keep))
    return (beta_t, abar_t)

def attend_head(operands):
    queries, keys_head, values_head = operands
    scores = jnp.dot(queries, keys_head.T, preferred_element_type=jnp.float32) * HEAD ** (-0.5)
    peak = lax.optimization_barrier(jnp.max(scores, axis=1, keepdims=True))
    probs = jnp.exp(scores - peak)
    totals = lax.optimization_barrier(jnp.sum(probs, axis=1, keepdims=True))
    mixed = jnp.dot(probs.astype(jnp.bfloat16), values_head, preferred_element_type=jnp.float32)
    return (mixed / totals).astype(jnp.bfloat16)

def reference(hidden, stream, w_query, w_key, w_value, w_out, out_gain, w_final, latents, noise, timestep):

    def project(inputs, weight):
        return jnp.dot(inputs, weight, preferred_element_type=jnp.float32).astype(jnp.bfloat16)

    def by_heads(flat):
        return flat.reshape(TOKENS, HEADS, HEAD).transpose(1, 0, 2)
    src_keys = by_heads(project(hidden[0], w_key))
    src_values = by_heads(project(hidden[0], w_value))
    beta_t, abar_t = plan(timestep)
    group_heads = HEADS // N_FSDP
    out_groups = w_out.reshape(N_FSDP, group_heads, HEAD, D)
    eps_all = []
    stepped_all = []
    for branch_id in range(2):
        queries = by_heads(project(hidden[branch_id], w_query))
        mixed = lax.map(attend_head, (queries, src_keys, src_values))
        mixed = mixed.reshape(N_FSDP, group_heads, TOKENS, HEAD)
        total = stream[branch_id].astype(jnp.float32)
        for slot in range(N_FSDP):
            term = jnp.einsum('hqd,hdn->qn', mixed[slot].astype(jnp.float32), out_groups[slot].astype(jnp.float32))
            total = total + lax.optimization_barrier(term.astype(jnp.bfloat16)).astype(jnp.float32)
        state = lax.optimization_barrier(total.astype(jnp.bfloat16)).astype(jnp.float32)
        inverse_rms = lax.rsqrt(lax.optimization_barrier(jnp.sum(state * state, axis=1, keepdims=True)) / D + 1e-06)
        eps_branch = jnp.dot(state * out_gain * inverse_rms, w_final, precision=lax.Precision.HIGHEST)
        moved = (latents[branch_id] - beta_t / jnp.sqrt(1.0 - abar_t) * eps_branch) / jnp.sqrt(1.0 - beta_t)
        eps_all.append(eps_branch)
        stepped_all.append(moved + jnp.sqrt(beta_t) * noise[branch_id])
    return (jnp.stack(eps_all), jnp.stack(stepped_all))
```

```python
import math

import jax
import jax.numpy as jnp
from jax import lax
from jax.experimental import pallas as pl
from jax.experimental.pallas import tpu as pltpu
from jax.sharding import PartitionSpec as P

D = 6144
HEAD = 128
STEPS = 1000
AXES = ("branch", "ctx", "fsdp")
SCORE_SCALE = HEAD ** (-0.5) * math.log2(math.e)
F32 = jnp.float32
BF16 = jnp.bfloat16


def line(b, y, z, l, x):
    return b * 128 + ((y % 4) * 4 + z % 4) * 8 + (l % 2) * 4 + x % 4


def fetch(value, source):
    route = []
    for b in range(2):
        for y in range(4):
            for z in range(4):
                for l in range(2):
                    for x in range(4):
                        found = source(b, y, z, l, x)
                        if found is not None:
                            route.append((line(*found), line(b, y, z, l, x)))
    return lax.ppermute(value, AXES, route)


def along(axis, step):
    def source(*device):
        moved = list(device)
        moved["byzlx".index(axis)] += step
        return moved

    return source


def swap_cores(value):
    return fetch(value, lambda b, y, z, l, x: (1 - b, y, z, l, x))


def ring(block, axis):
    half = block.shape[0] // 2
    ahead = fetch(block, along(axis, 1))
    behind = fetch(block, along(axis, -1))
    far_top = fetch(ahead[:half], along(axis, 1))
    far_bottom = fetch(behind[half:], along(axis, -1))
    return block, ahead, behind, far_top, far_bottom


def gather_all(piece):
    return ring(jnp.concatenate(ring(piece, "z"), axis=0), "y")


def whole_order(y, z):
    zs = [z, z + 1, z + 3, z + 2]
    return [
        jnp.stack([((y + dy) % 4) * 4 + zz % 4 for zz in part])
        for dy, part in ((0, zs), (1, zs), (3, zs), (2, zs[:2]), (2, zs[2:]))
    ]


def gather_half(piece, core):
    def first(b, y, z, l, x):
        sign = 1 - 2 * l
        return (b, y, z + sign if b == 0 else z - sign, l, x)

    def second(b, y, z, l, x):
        return (b, y, z - (1 - 2 * l), l, x) if b == 1 else None

    near = fetch(piece, first)
    far = fetch(near, second)
    both = jnp.where(
        core == 0, jnp.concatenate([piece, near], axis=0), jnp.concatenate([near, far], axis=0)
    )
    return ring(both, "y")


def half_order(y, z, l, core):
    sign = 1 - 2 * l
    zs = [jnp.where(core == 0, z, z - sign), jnp.where(core == 0, z + sign, z + 2)]
    return [
        jnp.stack([((y + dy) % 4) * 4 + (zz + 4) % 4 for zz in part])
        for dy, part in ((0, zs), (1, zs), (3, zs), (2, zs[:1]), (2, zs[1:]))
    ]


def project_kernel(order, x_ref, w_ref, *refs):
    out_ref = refs[-1]

    @pl.when(pl.program_id(0) == 0)
    def _():
        out_ref[...] = refs[0][...] if len(refs) == 2 else jnp.zeros_like(out_ref)

    out_ref[...] += jnp.dot(x_ref[...], w_ref[...], preferred_element_type=F32)


def project(x, weight, order, total=None):
    rows, cols, depth = x.shape[0], weight.shape[1], 384
    steps = weight.shape[0] // depth
    whole = pl.BlockSpec((rows, cols), lambda i, order: (0, 0))
    return pl.pallas_call(
        project_kernel,
        out_shape=jax.ShapeDtypeStruct((rows, cols), F32),
        grid_spec=pltpu.PrefetchScalarGridSpec(
            num_scalar_prefetch=1,
            grid=(steps,),
            in_specs=[
                pl.BlockSpec((rows, depth), lambda i, order: (0, order[i])),
                pl.BlockSpec((depth, cols), lambda i, order: (i, 0)),
            ]
            + ([whole] if total is not None else []),
            out_specs=whole,
        ),
        compiler_params=pltpu.CompilerParams(vmem_limit_bytes=16 * 2**20),
        cost_estimate=pl.CostEstimate(
            flops=2 * rows * cols * weight.shape[0],
            bytes_accessed=2 * (rows + cols) * weight.shape[0] + 8 * rows * cols,
            transcendentals=0,
        ),
        name="project",
    )(order, x, weight, *([total] if total is not None else []))


def project_all(x, weights, orders):
    total = None
    for weight, order in zip(weights, orders):
        total = project(x, weight, order, total)
    return total


def attend_kernel(n_pairs, first, last, core, q_ref, *refs):
    pairs, refs = refs[: 2 * n_pairs], refs[2 * n_pairs :]
    if not first:
        carried, refs = refs[:3], refs[3:]
    outs, refs = (refs[:1], refs[1:]) if last else (refs[:3], refs[3:])
    keys, values, peaks, sums, acc, sems = refs

    def move(k_at, v_at):
        begin = 0
        copies = []
        for i in range(n_pairs):
            rows = pairs[2 * i].shape[0]
            span = pl.ds(begin, rows)
            copies.append(pltpu.make_async_copy(pairs[2 * i + k_at], keys.at[span], sems.at[2 * i]))
            copies.append(
                pltpu.make_async_copy(pairs[2 * i + v_at], values.at[span], sems.at[2 * i + 1])
            )
            begin += rows
        for copy in copies:
            copy.start()
        for copy in copies:
            copy.wait()

    @pl.when(core[0] == 0)
    def _():
        move(0, 1)

    @pl.when(core[0] != 0)
    def _():
        move(1, 0)

    n_keys, chunk = keys.shape[0], 768
    heads = q_ref.shape[1] // HEAD
    for h in range(heads):
        lanes = slice(h * HEAD, (h + 1) * HEAD)
        query = q_ref[:, lanes]
        if first:
            peak = jnp.full((query.shape[0], 1), -jnp.inf, F32)
            total = jnp.zeros((query.shape[0], 1), F32)
            mixed = jnp.zeros((query.shape[0], HEAD), F32)
        else:
            peak, total, mixed = carried[0][h], carried[1][h], carried[2][:, lanes]
        for begin in range(0, n_keys, chunk):
            span = slice(begin, begin + chunk)
            scores = (
                lax.dot_general(
                    query,
                    keys[span, lanes],
                    (((1,), (1,)), ((), ())),
                    preferred_element_type=F32,
                )
                * SCORE_SCALE
            )
            new_peak = jnp.maximum(peak, jnp.max(scores, axis=1, keepdims=True))
            factor = jnp.exp2(peak - new_peak)
            probs = jnp.exp2(scores - new_peak)
            total = total * factor + jnp.sum(probs, axis=1, keepdims=True)
            mixed = mixed * factor + jnp.dot(
                probs.astype(BF16), values[span, lanes], preferred_element_type=F32
            )
            peak = new_peak
        if last:
            outs[0][:, lanes] = (mixed / total).astype(BF16)
        else:
            outs[0][h], outs[1][h], outs[2][:, lanes] = peak, total, mixed


def attend(core, query, pairs, carried, last):
    rows, width = query.shape
    heads = width // HEAD
    n_keys = sum(mine.shape[0] for mine, _ in pairs)
    state = [
        jax.ShapeDtypeStruct((heads, rows, 1), F32),
        jax.ShapeDtypeStruct((heads, rows, 1), F32),
        jax.ShapeDtypeStruct((rows, width), F32),
    ]
    in_vmem = pl.BlockSpec(memory_space=pltpu.VMEM)
    flat = [array for pair in pairs for array in pair]
    kernel = lambda *refs: attend_kernel(len(pairs), carried is None, last, *refs)
    return pl.pallas_call(
        kernel,
        out_shape=jax.ShapeDtypeStruct((rows, width), BF16) if last else state,
        grid_spec=pltpu.PrefetchScalarGridSpec(
            num_scalar_prefetch=1,
            grid=(1,),
            in_specs=[in_vmem]
            + [pl.BlockSpec(memory_space=pl.ANY)] * len(flat)
            + ([in_vmem] * 3 if carried is not None else []),
            out_specs=in_vmem if last else [in_vmem] * 3,
            scratch_shapes=[
                pltpu.VMEM((n_keys, width), BF16),
                pltpu.VMEM((n_keys, width), BF16),
                pltpu.VMEM((8, 128), F32),
                pltpu.VMEM((8, 128), F32),
                pltpu.VMEM((8, 128), F32),
                pltpu.SemaphoreType.DMA((len(flat),)),
            ],
        ),
        compiler_params=pltpu.CompilerParams(vmem_limit_bytes=40 * 2**20),
        cost_estimate=pl.CostEstimate(
            flops=4 * rows * width * n_keys,
            bytes_accessed=4 * n_keys * width,
            transcendentals=rows * heads * n_keys,
        ),
        name="attend",
    )(core, query, *flat, *(carried if carried is not None else []))


def reorder_kernel(places, *refs):
    sources, out, sems = refs[:-2], refs[-2], refs[-1]
    copies = []
    for source in sources:
        for begin in range(0, source.shape[0], 192):
            i = len(copies)
            place = pl.multiple_of(places[i] * 192, 192)
            copies.append(
                pltpu.make_async_copy(
                    source.at[pl.ds(begin, 192)], out.at[pl.ds(place, 192)], sems.at[i]
                )
            )
    for copy in copies:
        copy.start()
    for copy in copies:
        copy.wait()


def reorder(arrays, places):
    return pl.pallas_call(
        reorder_kernel,
        out_shape=jax.ShapeDtypeStruct((3072, 768), BF16),
        grid_spec=pltpu.PrefetchScalarGridSpec(
            num_scalar_prefetch=1,
            grid=(1,),
            in_specs=[pl.BlockSpec(memory_space=pl.ANY)] * len(arrays),
            out_specs=pl.BlockSpec(memory_space=pl.ANY),
            scratch_shapes=[pltpu.SemaphoreType.DMA((16,))],
        ),
        cost_estimate=pl.CostEstimate(flops=0, bytes_accessed=4 * 3072 * 768, transcendentals=0),
        name="reorder",
    )(places, *arrays)


def spread_out(w_out, c):
    parts = []
    for k in range(2):

        def source(b, y, z, l, x, k=k):
            ctx, fsdp = y * 4 + z, l * 4 + x
            from_ctx, from_fsdp = 2 * fsdp + ((ctx % 2) ^ k), ctx // 2
            return (b, from_ctx // 4, from_ctx % 4, from_fsdp // 4, from_fsdp % 4)

        upper = (c % 2) != k
        sent = jnp.where(upper, w_out[192:], w_out[:192])
        parts.append(fetch(sent, source))
    even = c % 2 == 0
    return jnp.where(
        even, jnp.concatenate(parts, axis=1), jnp.concatenate(parts[::-1], axis=1)
    )


def plan(timestep):
    step_index = jnp.arange(STEPS, dtype=jnp.int32)
    betas = 0.0001 + (0.02 - 0.0001) * step_index.astype(jnp.float32) / (STEPS - 1)
    log_keep = jnp.cumsum(jnp.log1p(-betas))
    picked = (step_index == timestep[0]).astype(jnp.float32)
    beta_t = jnp.sum(picked * betas)
    abar_t = jnp.exp(jnp.sum(picked * log_keep))
    return (beta_t, abar_t)


def body(
    hidden, stream, w_query, w_key, w_value, w_out, out_gain, w_final, latents, noise, timestep
):
    inputs = hidden[0]
    core, c, f = (lax.axis_index(name) for name in AXES)
    y, z, l, x = c // 4, c % 4, f // 4, f % 4
    core_id = core.reshape(1).astype(jnp.int32)

    kv_weights = gather_all(jnp.where(core == 0, w_key, w_value))
    source = jnp.where(core == 0, inputs, fetch(inputs, lambda b, *at: (0, *at) if b else None))
    kv = project_all(source, kv_weights, whole_order(y, z)).astype(BF16)

    mine = gather_half(w_query, core)
    query_weights = mine + tuple(swap_cores(part) for part in mine)
    query_orders = half_order(y, z, l, core) + half_order(y, z, l, 1 - core)
    query = project_all(inputs, query_weights, query_orders).astype(BF16)

    kv_parts = gather_all(kv)
    pairs = [(part, swap_cores(part)) for part in kv_parts]
    carried = attend(core_id, query, pairs[:1], None, False)
    carried = attend(core_id, query, pairs[1:3], carried, False)
    mixed = attend(core_id, query, pairs[3:], carried, True)

    mine = gather_half(spread_out(w_out, c), core)
    out_parts = mine + tuple(swap_cores(part) for part in mine)
    rows_from = jnp.concatenate(half_order(y, z, l, core) + half_order(y, z, l, 1 - core))
    group = rows_from // 2
    offset = (group // 4 + l) % 2 * 4 + (group % 4 - x + 4) % 4
    slot = jnp.array([0, 1, 3, 2], jnp.int32)[offset % 4] * 2 + offset // 4
    out_rows = reorder(out_parts, (slot * 2 + rows_from % 2).astype(jnp.int32))

    pair = jnp.concatenate([mixed, fetch(mixed, along("l", 1))], axis=0)
    groups = jnp.concatenate(ring(pair, "x"), axis=0).reshape(8, 384, 384)
    term = jnp.einsum(
        "gqk,gkn->qn", groups, out_rows.reshape(8, 384, 768), preferred_element_type=F32
    )
    state = lax.optimization_barrier((stream[0].astype(F32) + term).astype(BF16)).astype(F32)
    squares = jnp.sum(state * state, axis=1, keepdims=True)
    part = jnp.dot(state * out_gain, w_final, precision=lax.Precision.HIGHEST)

    def pack(part, squares):
        high = squares.astype(BF16)
        low = (squares - high.astype(F32)).astype(BF16)
        pad = jnp.zeros((part.shape[0], 62), BF16)
        return jnp.concatenate([part.astype(BF16), high, low, pad], axis=1)

    def unpack(packed):
        wide = packed.astype(F32)
        return wide[:, :64], wide[:, 64:65] + wide[:, 65:66]

    def add(*values):
        return tuple(sum(column) for column in zip(*values))

    here = (part, squares)
    here = add(here, unpack(fetch(pack(*here), along("l", 1))))
    packed = pack(*here)
    eps_sum, square_total = add(here, *(unpack(fetch(packed, along("x", step))) for step in (1, 2, 3)))
    eps_branch = eps_sum * lax.rsqrt(square_total / D + 1e-06)
    beta_t, abar_t = plan(timestep)
    moved = (latents[0] - beta_t / jnp.sqrt(1.0 - abar_t) * eps_branch) / jnp.sqrt(1.0 - beta_t)
    stepped = moved + jnp.sqrt(beta_t) * noise[0]
    return (eps_branch[None], stepped[None])


def solution(mesh):
    return jax.shard_map(
        body,
        mesh=mesh,
        in_specs=(
            P("branch", "ctx", None),
            P("branch", "ctx", "fsdp"),
            P("ctx", "fsdp"),
            P("ctx", "fsdp"),
            P("ctx", "fsdp"),
            P("fsdp", "ctx"),
            P("fsdp"),
            P("fsdp", None),
            P("branch", "ctx", None),
            P("branch", "ctx", None),
            P(),
        ),
        out_specs=(P("branch", "ctx", None), P("branch", "ctx", None)),
        check_vma=False,
    )
```

```python
import math

import jax
import jax.numpy as jnp
from jax import lax
from jax.experimental import pallas as pl
from jax.experimental.pallas import tpu as pltpu
from jax.sharding import PartitionSpec as P

D = 6144
HEAD = 128
STEPS = 1000
AXES = ("branch", "ctx", "fsdp")
SCORE_SCALE = HEAD ** (-0.5) * math.log2(math.e)
F32 = jnp.float32
BF16 = jnp.bfloat16


def line(b, y, z, l, x):
    return b * 128 + ((y % 4) * 4 + z % 4) * 8 + (l % 2) * 4 + x % 4


def fetch(value, source):
    route = []
    for b in range(2):
        for y in range(4):
            for z in range(4):
                for l in range(2):
                    for x in range(4):
                        found = source(b, y, z, l, x)
                        if found is not None:
                            route.append((line(*found), line(b, y, z, l, x)))
    return lax.ppermute(value, AXES, route)


def along(axis, step):
    def source(*device):
        moved = list(device)
        moved["byzlx".index(axis)] += step
        return moved

    return source


def swap_cores(value):
    return fetch(value, lambda b, y, z, l, x: (1 - b, y, z, l, x))


def after(value, *others):
    return lax.optimization_barrier((value, *others))[0]


def ring(block, axis, gate=()):
    half = block.shape[0] // 2
    ahead = fetch(block, along(axis, 1))
    behind = fetch(block, along(axis, -1))
    if gate:
        ahead, behind = lax.optimization_barrier((ahead, behind, *gate))[:2]
    far_top = fetch(ahead[:half], along(axis, 1))
    far_bottom = fetch(behind[half:], along(axis, -1))
    return [block, ahead, behind, far_top, far_bottom]


def join_kernel(*refs):
    sources, out, sems = refs[:-2], refs[-2], refs[-1]
    copies, begin = [], 0
    for i, source in enumerate(sources):
        rows = source.shape[0]
        copies.append(pltpu.make_async_copy(source, out.at[pl.ds(begin, rows)], sems.at[i]))
        begin += rows
    for copy in copies:
        copy.start()
    for copy in copies:
        copy.wait()


def join(arrays):
    rows = sum(array.shape[0] for array in arrays)
    shape = (rows, arrays[0].shape[1])
    return pl.pallas_call(
        join_kernel,
        out_shape=jax.ShapeDtypeStruct(shape, arrays[0].dtype),
        in_specs=[pl.BlockSpec(memory_space=pl.ANY)] * len(arrays),
        out_specs=pl.BlockSpec(memory_space=pltpu.VMEM),
        scratch_shapes=[pltpu.SemaphoreType.DMA((len(arrays),))],
        compiler_params=pltpu.CompilerParams(vmem_limit_bytes=8 * 2**20),
        cost_estimate=pl.CostEstimate(
            flops=0, bytes_accessed=4 * shape[0] * shape[1], transcendentals=0
        ),
        name="join",
    )(*arrays)


def all_order(y, z):
    at = lambda dy, dz: ((y + dy) % 4) * 4 + (z + dz) % 4
    return [
        [at(dy, 0) for dy in (0, 1, 3, 2)],
        [at(0, dz) for dz in (1, 3, 2)],
        [at(dy, dz) for dy in (1, 3) for dz in (1, 3, 2)],
        [at(2, dz) for dz in (1, 3, 2)],
    ]


def gather_half(piece, core, axes):
    at = "byzlx".index(axes[0])

    def moved(device, step):
        device = list(device)
        device[at] += step * (1 - 2 * device[3])
        return device

    near = fetch(piece, lambda *device: moved(device, 1 if device[0] == 0 else -1))
    far = fetch(near, lambda *device: moved(device, -1) if device[0] == 1 else None)
    both = jnp.where(
        core == 0, jnp.concatenate([piece, near], axis=0), jnp.concatenate([near, far], axis=0)
    )
    return both, far


def half_order(y, z, l, core, axes):
    sign = 1 - 2 * l
    low = jnp.where(core == 0, 0, -sign)
    high = jnp.where(core == 0, sign, 2)
    places = [(step, near) for step in (0, 1, 3, 2) for near in (low, high)]
    if axes == "yz":
        return [((y + near + 4) % 4) * 4 + (z + step) % 4 for step, near in places]
    return [((y + step) % 4) * 4 + (z + near + 4) % 4 for step, near in places]


def project_kernel(n_weights, order, x_ref, *refs):
    weights, refs = refs[:n_weights], refs[n_weights:]
    totals, (out_ref, x_all, w_all, sems) = refs[:-4], refs[-4:]
    copies = []
    for i in range(w_all.shape[0] // 384):
        place = pl.multiple_of(order[i] * 384, 128)
        copies.append((x_ref.at[:, pl.ds(place, 384)], x_all.at[:, pl.ds(i * 384, 384)]))
    begin = 0
    for weight in weights:
        copies.append((weight, w_all.at[pl.ds(begin, weight.shape[0])]))
        begin += weight.shape[0]
    copies = [pltpu.make_async_copy(*ends, sems.at[i]) for i, ends in enumerate(copies)]
    for copy in copies:
        copy.start()
    for copy in copies:
        copy.wait()
    total = jnp.dot(x_all[...], w_all[...], preferred_element_type=F32)
    if totals:
        total += totals[0][...]
    out_ref[...] = total.astype(out_ref.dtype)


def project(x, weights, order, total, dtype):
    rows, cols = x.shape[0], weights[0].shape[1]
    depth = sum(weight.shape[0] for weight in weights)
    in_vmem, anywhere = (pl.BlockSpec(memory_space=space) for space in (pltpu.VMEM, pl.ANY))
    return pl.pallas_call(
        lambda *refs: project_kernel(len(weights), *refs),
        out_shape=jax.ShapeDtypeStruct((rows, cols), dtype),
        grid_spec=pltpu.PrefetchScalarGridSpec(
            num_scalar_prefetch=1,
            grid=(1,),
            in_specs=[anywhere] * (1 + len(weights)) + [in_vmem] * (total is not None),
            out_specs=in_vmem,
            scratch_shapes=[
                pltpu.VMEM((rows, depth), BF16),
                pltpu.VMEM((depth, cols), BF16),
                pltpu.SemaphoreType.DMA((depth // 384 + len(weights),)),
            ],
        ),
        compiler_params=pltpu.CompilerParams(vmem_limit_bytes=32 * 2**20),
        cost_estimate=pl.CostEstimate(
            flops=2 * rows * cols * depth,
            bytes_accessed=2 * (rows + cols) * depth + 8 * rows * cols,
            transcendentals=0,
        ),
        name="project",
    )(jnp.stack(order).astype(jnp.int32), x, *weights, *([total] if total is not None else []))


def project_all(x, parts, orders):
    total = None
    for i, (part, order) in enumerate(zip(parts, orders)):
        total = project(x, part, order, total, BF16 if i + 1 == len(parts) else F32)
    return total


def attend_kernel(n_pairs, first, last, core, q_ref, *refs):
    pairs, refs = refs[: 2 * n_pairs], refs[2 * n_pairs :]
    if not first:
        carried, refs = refs[:3], refs[3:]
    outs, refs = (refs[:1], refs[1:]) if last else (refs[:3], refs[3:])
    keys, values, peaks, sums, acc, sems = refs

    def move(k_at, v_at):
        begin = 0
        copies = []
        for i in range(n_pairs):
            rows = pairs[2 * i].shape[0]
            span = pl.ds(begin, rows)
            copies.append(pltpu.make_async_copy(pairs[2 * i + k_at], keys.at[span], sems.at[2 * i]))
            copies.append(
                pltpu.make_async_copy(pairs[2 * i + v_at], values.at[span], sems.at[2 * i + 1])
            )
            begin += rows
        for copy in copies:
            copy.start()
        for copy in copies:
            copy.wait()

    @pl.when(core[0] == 0)
    def _():
        move(0, 1)

    @pl.when(core[0] != 0)
    def _():
        move(1, 0)

    n_keys = keys.shape[0]
    chunk = 768 if n_keys % 768 == 0 else 576
    heads = q_ref.shape[1] // HEAD
    for h in range(heads):
        lanes = slice(h * HEAD, (h + 1) * HEAD)
        query = q_ref[:, lanes]
        if first:
            peak = jnp.full((query.shape[0], 1), -jnp.inf, F32)
            total = jnp.zeros((query.shape[0], 1), F32)
            mixed = jnp.zeros((query.shape[0], HEAD), F32)
        else:
            peak, total, mixed = carried[0][h], carried[1][h], carried[2][:, lanes]
        for begin in range(0, n_keys, chunk):
            span = slice(begin, begin + chunk)
            scores = (
                lax.dot_general(
                    query,
                    keys[span, lanes],
                    (((1,), (1,)), ((), ())),
                    preferred_element_type=F32,
                )
                * SCORE_SCALE
            )
            new_peak = jnp.maximum(peak, jnp.max(scores, axis=1, keepdims=True))
            factor = jnp.exp2(peak - new_peak)
            probs = jnp.exp2(scores - new_peak)
            total = total * factor + jnp.sum(probs, axis=1, keepdims=True)
            mixed = mixed * factor + jnp.dot(
                probs.astype(BF16), values[span, lanes], preferred_element_type=F32
            )
            peak = new_peak
        if last:
            outs[0][:, lanes] = (mixed / total).astype(BF16)
        else:
            outs[0][h], outs[1][h], outs[2][:, lanes] = peak, total, mixed


def attend(core, query, pairs, carried, last):
    rows, width = query.shape
    heads = width // HEAD
    n_keys = sum(mine.shape[0] for mine, _ in pairs)
    state = [
        jax.ShapeDtypeStruct((heads, rows, 1), F32),
        jax.ShapeDtypeStruct((heads, rows, 1), F32),
        jax.ShapeDtypeStruct((rows, width), F32),
    ]
    in_vmem = pl.BlockSpec(memory_space=pltpu.VMEM)
    flat = [array for pair in pairs for array in pair]
    kernel = lambda *refs: attend_kernel(len(pairs), carried is None, last, *refs)
    return pl.pallas_call(
        kernel,
        out_shape=jax.ShapeDtypeStruct((rows, width), BF16) if last else state,
        grid_spec=pltpu.PrefetchScalarGridSpec(
            num_scalar_prefetch=1,
            grid=(1,),
            in_specs=[in_vmem]
            + [pl.BlockSpec(memory_space=pl.ANY)] * len(flat)
            + ([in_vmem] * 3 if carried is not None else []),
            out_specs=in_vmem if last else [in_vmem] * 3,
            scratch_shapes=[
                pltpu.VMEM((n_keys, width), BF16),
                pltpu.VMEM((n_keys, width), BF16),
                pltpu.VMEM((8, 128), F32),
                pltpu.VMEM((8, 128), F32),
                pltpu.VMEM((8, 128), F32),
                pltpu.SemaphoreType.DMA((len(flat),)),
            ],
        ),
        compiler_params=pltpu.CompilerParams(vmem_limit_bytes=40 * 2**20),
        cost_estimate=pl.CostEstimate(
            flops=4 * rows * width * n_keys,
            bytes_accessed=4 * n_keys * width,
            transcendentals=rows * heads * n_keys,
        ),
        name="attend",
    )(core, query, *flat, *(carried if carried is not None else []))


def reorder_kernel(places, *refs):
    sources, out, sems = refs[:-2], refs[-2], refs[-1]
    copies = []
    for source in sources:
        for begin in range(0, source.shape[0], 192):
            i = len(copies)
            place = pl.multiple_of(places[i] * 192, 192)
            copies.append(
                pltpu.make_async_copy(
                    source.at[pl.ds(begin, 192)], out.at[pl.ds(place, 192)], sems.at[i]
                )
            )
    for copy in copies:
        copy.start()
    for copy in copies:
        copy.wait()


def reorder(arrays, places):
    return pl.pallas_call(
        reorder_kernel,
        out_shape=jax.ShapeDtypeStruct((3072, 768), BF16),
        grid_spec=pltpu.PrefetchScalarGridSpec(
            num_scalar_prefetch=1,
            grid=(1,),
            in_specs=[pl.BlockSpec(memory_space=pl.ANY)] * len(arrays),
            out_specs=pl.BlockSpec(memory_space=pltpu.VMEM),
            scratch_shapes=[pltpu.SemaphoreType.DMA((16,))],
        ),
        compiler_params=pltpu.CompilerParams(vmem_limit_bytes=16 * 2**20),
        cost_estimate=pl.CostEstimate(flops=0, bytes_accessed=4 * 3072 * 768, transcendentals=0),
        name="reorder",
    )(places, *arrays)


def spread_out(w_out, c):
    parts = []
    for k in range(2):

        def source(b, y, z, l, x, k=k):
            ctx, fsdp = y * 4 + z, l * 4 + x
            from_ctx, from_fsdp = 2 * fsdp + ((ctx % 2) ^ k), ctx // 2
            return (b, from_ctx // 4, from_ctx % 4, from_fsdp // 4, from_fsdp % 4)

        upper = (c % 2) != k
        sent = jnp.where(upper, w_out[192:], w_out[:192])
        parts.append(fetch(sent, source))
    even = c % 2 == 0
    return jnp.where(
        even, jnp.concatenate(parts, axis=1), jnp.concatenate(parts[::-1], axis=1)
    )


def pack(wide):
    squares = wide[:, 64:65] + wide[:, 65:66]
    high = squares.astype(BF16).astype(F32)
    lane = lax.broadcasted_iota(jnp.int32, wide.shape, 1)
    return jnp.where(lane == 64, high, jnp.where(lane == 65, squares - high, wide)).astype(BF16)


def finish_kernel(n_groups, *refs):
    groups, refs = refs[:n_groups], refs[n_groups:]
    rows_ref, stream_ref, gain_ref, final_ref, wide_ref, packed_ref, mixed, sems = refs
    tokens = mixed.shape[0]
    copies = []
    for group in groups:
        for begin in range(0, group.shape[0], tokens):
            i = len(copies)
            place = mixed.at[:, pl.ds(i * 384, 384)]
            copies.append(pltpu.make_async_copy(group.at[pl.ds(begin, tokens)], place, sems.at[i]))
    for copy in copies:
        copy.start()
    for copy in copies:
        copy.wait()
    term = jnp.dot(mixed[...], rows_ref[...], preferred_element_type=F32)
    state = (stream_ref[...].astype(F32) + term).astype(BF16).astype(F32)
    squares = jnp.sum(state * state, axis=1, keepdims=True)
    part = jnp.dot(
        state * gain_ref[...],
        final_ref[...],
        precision=lax.Precision.HIGHEST,
        preferred_element_type=F32,
    )
    lane = lax.broadcasted_iota(jnp.int32, part.shape, 1)
    wide = jnp.where(lane == 64, squares, part)
    wide_ref[...] = wide
    packed_ref[...] = pack(wide)


def finish(groups, rows, stream, gain, final):
    tokens, depth = stream.shape[0], rows.shape[0]
    in_vmem = pl.BlockSpec(memory_space=pltpu.VMEM)
    return pl.pallas_call(
        lambda *refs: finish_kernel(len(groups), *refs),
        out_shape=[jax.ShapeDtypeStruct((tokens, 128), dtype) for dtype in (F32, BF16)],
        in_specs=[pl.BlockSpec(memory_space=pl.ANY)] * len(groups) + [in_vmem] * 4,
        out_specs=[in_vmem] * 2,
        scratch_shapes=[
            pltpu.VMEM((tokens, depth), BF16),
            pltpu.SemaphoreType.DMA((depth // 384,)),
        ],
        compiler_params=pltpu.CompilerParams(vmem_limit_bytes=40 * 2**20),
        cost_estimate=pl.CostEstimate(
            flops=2 * tokens * depth * rows.shape[1],
            bytes_accessed=2 * depth * (tokens + rows.shape[1]),
            transcendentals=0,
        ),
        name="finish",
    )(*groups, rows, stream, gain[None], jnp.pad(final, ((0, 0), (0, 64))))


def plan(timestep):
    step_index = jnp.arange(STEPS, dtype=jnp.int32)
    betas = 0.0001 + (0.02 - 0.0001) * step_index.astype(jnp.float32) / (STEPS - 1)
    log_keep = jnp.cumsum(jnp.log1p(-betas))
    picked = (step_index == timestep[0]).astype(jnp.float32)
    beta_t = jnp.sum(picked * betas)
    abar_t = jnp.exp(jnp.sum(picked * log_keep))
    return (beta_t, abar_t)


def body(
    hidden, stream, w_query, w_key, w_value, w_out, out_gain, w_final, latents, noise, timestep
):
    inputs = hidden[0]
    core, c, f = (lax.axis_index(name) for name in AXES)
    y, z, l, x = c // 4, c % 4, f // 4, f % 4
    core_id = core.reshape(1).astype(jnp.int32)

    weight = jnp.where(core == 0, w_key, w_value)
    near_weights = ring(weight, "y")
    source = jnp.where(core == 0, inputs, fetch(inputs, lambda b, *at: (0, *at) if b else None))
    other_z = join(ring(weight, "z")[1:])
    query_block, query_far = gather_half(w_query, core, "yz")
    query_ring = ring(after(query_block, other_z), "z")
    other_z = after(other_z, *near_weights[3:], query_far)
    _, *far_weights = ring(other_z, "y")
    weights = [near_weights, [other_z], far_weights[:2], far_weights[2:]]
    weights[3] = [after(part, *query_ring[1:3]) for part in weights[3]]
    kv = project_all(source, weights, all_order(y, z))
    spread = spread_out(after(w_out, kv), c)

    near_kv = ring(kv, "y")
    other_z = join(ring(kv, "z")[1:])
    out_block, _ = gather_half(after(spread, other_z), core, "zy")
    other_z = after(other_z, *near_kv[3:], *query_ring[3:])
    query_weights = [query_ring, [swap_cores(part) for part in query_ring]]
    query_orders = [half_order(y, z, l, side, "yz") for side in (core, 1 - core)]
    query = project_all(inputs, query_weights, query_orders)

    def attend_to(parts, carried, last=False):
        pairs = [(part, swap_cores(part)) for part in parts]
        return attend(core_id, query, pairs, carried, last)

    carried = attend_to([other_z], attend_to(near_kv, None))
    _, *far_kv = ring(other_z, "y", carried)
    carried = attend_to(far_kv[:2], carried)
    mixed = attend_to(far_kv[2:], carried, True)

    mine = ring(after(out_block, *far_kv[2:]), "y")
    out_parts = mine + [swap_cores(part) for part in mine]
    rows_from = jnp.stack(
        half_order(y, z, l, core, "zy") + half_order(y, z, l, 1 - core, "zy")
    )
    group = rows_from // 2
    offset = (group // 4 + l) % 2 * 4 + (group % 4 - x + 4) % 4
    step = offset % 4
    slot = jnp.where(step < 2, step, 5 - step) * 2 + offset // 4
    out_rows = reorder(out_parts, (slot * 2 + rows_from % 2).astype(jnp.int32))

    groups = ring(join([mixed, fetch(mixed, along("l", 1))]), "x")
    wide, packed = finish(groups, out_rows, stream[0], out_gain, w_final)
    wide += fetch(packed, along("l", 1)).astype(F32)
    packed = pack(wide)
    wide += sum(fetch(packed, along("x", step)).astype(F32) for step in (1, 2, 3))
    square_total = wide[:, 64:65] + wide[:, 65:66]
    eps_branch = wide[:, :64] * lax.rsqrt(square_total / D + 1e-06)
    beta_t, abar_t = plan(timestep)
    moved = (latents[0] - beta_t / jnp.sqrt(1.0 - abar_t) * eps_branch) / jnp.sqrt(1.0 - beta_t)
    stepped = moved + jnp.sqrt(beta_t) * noise[0]
    return (eps_branch[None], stepped[None])


def solution(mesh):
    return jax.shard_map(
        body,
        mesh=mesh,
        in_specs=(
            P("branch", "ctx", None),
            P("branch", "ctx", "fsdp"),
            P("ctx", "fsdp"),
            P("ctx", "fsdp"),
            P("ctx", "fsdp"),
            P("fsdp", "ctx"),
            P("fsdp"),
            P("fsdp", None),
            P("branch", "ctx", None),
            P("branch", "ctx", None),
            P(),
        ),
        out_specs=(P("branch", "ctx", None), P("branch", "ctx", None)),
        check_vma=False,
    )
```

```python
import math

import jax
import jax.numpy as jnp
from jax import lax
from jax.experimental import pallas as pl
from jax.experimental.pallas import tpu as pltpu
from jax.sharding import PartitionSpec as P

D = 6144
HEAD = 128
STEPS = 1000
AXES = ("branch", "ctx", "fsdp")
SCORE_SCALE = HEAD ** (-0.5) * math.log2(math.e)
VMEM_BYTES = 16 * 2**20
F32 = jnp.float32
BF16 = jnp.bfloat16


def line(b, y, z, l, x):
    return b * 128 + ((y % 4) * 4 + z % 4) * 8 + (l % 2) * 4 + x % 4


def fetch(value, source):
    route = []
    for b in range(2):
        for y in range(4):
            for z in range(4):
                for l in range(2):
                    for x in range(4):
                        found = source(b, y, z, l, x)
                        if found is not None:
                            route.append((line(*found), line(b, y, z, l, x)))
    return lax.ppermute(value, AXES, route)


def along(axis, step):
    def source(*device):
        moved = list(device)
        moved["byzlx".index(axis)] += step
        return moved

    return source


def swap_cores(value):
    return fetch(value, lambda b, y, z, l, x: (1 - b, y, z, l, x))


def together(*values):
    return lax.optimization_barrier(values)


def from_y(value, step):
    return fetch(value, along("y", step))


def from_z(value, step):
    return fetch(value, along("z", step))


def join_kernel(*refs):
    sources, out, sems = refs[:-2], refs[-2], refs[-1]
    copies, begin = [], 0
    for i, source in enumerate(sources):
        rows = source.shape[0]
        copies.append(pltpu.make_async_copy(source, out.at[pl.ds(begin, rows)], sems.at[i]))
        begin += rows
    for copy in copies:
        copy.start()
    for copy in copies:
        copy.wait()


def join(arrays):
    shape = (sum(array.shape[0] for array in arrays), arrays[0].shape[1])
    return pl.pallas_call(
        join_kernel,
        out_shape=jax.ShapeDtypeStruct(shape, arrays[0].dtype),
        in_specs=[pl.BlockSpec(memory_space=pl.ANY)] * len(arrays),
        out_specs=pl.BlockSpec(memory_space=pltpu.VMEM),
        scratch_shapes=[pltpu.SemaphoreType.DMA((len(arrays),))],
        compiler_params=pltpu.CompilerParams(vmem_limit_bytes=8 * 2**20),
        cost_estimate=pl.CostEstimate(
            flops=0, bytes_accessed=4 * shape[0] * shape[1], transcendentals=0
        ),
        name="join",
    )(*arrays)


def near_of(axis):
    def source(*device):
        device = list(device)
        step = 1 - 2 * device[3]
        device["byzlx".index(axis)] += step if device[0] == 0 else -step
        return device

    return source


def far_of(axis):
    return lambda *device: along(axis, 2)(*device) if device[0] == 1 else None


def pair_of(core, piece, near, far):
    return jnp.where(
        core == 0, jnp.concatenate([piece, near], axis=0), jnp.concatenate([near, far], axis=0)
    )


def pair_order(y, z, l, core, axis, steps):
    sign = 1 - 2 * l
    low = jnp.where(core == 0, 0, -sign)
    high = jnp.where(core == 0, sign, 2)
    places = [(step, near) for step in steps for near in (low, high)]
    if axis == "y":
        return [((y + near + 4) % 4) * 4 + (z + step) % 4 for step, near in places]
    return [((y + step) % 4) * 4 + (z + near + 4) % 4 for step, near in places]


def project_kernel(n_weights, order, x_ref, *refs):
    weights, refs = refs[:n_weights], refs[n_weights:]
    totals, (out_ref, x_all, w_all, sems) = refs[:-4], refs[-4:]
    copies = []
    for i in range(w_all.shape[0] // 384):
        place = pl.multiple_of(order[i] * 384, 128)
        copies.append((x_ref.at[:, pl.ds(place, 384)], x_all.at[:, pl.ds(i * 384, 384)]))
    begin = 0
    for weight in weights:
        copies.append((weight, w_all.at[pl.ds(begin, weight.shape[0])]))
        begin += weight.shape[0]
    copies = [pltpu.make_async_copy(*ends, sems.at[i]) for i, ends in enumerate(copies)]
    for copy in copies:
        copy.start()
    for copy in copies:
        copy.wait()
    total = jnp.dot(x_all[...], w_all[...], preferred_element_type=F32)
    if totals:
        total += totals[0][...]
    out_ref[...] = total.astype(out_ref.dtype)


def project(x, weights, order, total, dtype):
    rows, cols = x.shape[0], weights[0].shape[1]
    depth = sum(weight.shape[0] for weight in weights)
    in_vmem, anywhere = (pl.BlockSpec(memory_space=space) for space in (pltpu.VMEM, pl.ANY))
    return pl.pallas_call(
        lambda *refs: project_kernel(len(weights), *refs),
        out_shape=jax.ShapeDtypeStruct((rows, cols), dtype),
        grid_spec=pltpu.PrefetchScalarGridSpec(
            num_scalar_prefetch=1,
            grid=(1,),
            in_specs=[anywhere] * (1 + len(weights)) + [in_vmem] * (total is not None),
            out_specs=in_vmem,
            scratch_shapes=[
                pltpu.VMEM((rows, depth), BF16),
                pltpu.VMEM((depth, cols), BF16),
                pltpu.SemaphoreType.DMA((depth // 384 + len(weights),)),
            ],
        ),
        compiler_params=pltpu.CompilerParams(vmem_limit_bytes=VMEM_BYTES),
        cost_estimate=pl.CostEstimate(
            flops=2 * rows * cols * depth,
            bytes_accessed=2 * (rows + cols) * depth + 8 * rows * cols,
            transcendentals=0,
        ),
        name="project",
    )(jnp.stack(list(order)).astype(jnp.int32), x, *weights, *([total] if total is not None else []))


def attend_kernel(n_pairs, first, last, core, q_ref, *refs):
    pairs, refs = refs[: 2 * n_pairs], refs[2 * n_pairs :]
    if not first:
        carried, refs = refs[:2], refs[2:]
    outs, refs = (refs[:1], refs[1:]) if last else (refs[:2], refs[2:])
    kv, sems = refs
    copies, begin = [], 0
    for i in range(n_pairs):
        rows = pairs[2 * i].shape[0]
        for j, side in enumerate((core[0], 1 - core[0])):
            copies.append(
                pltpu.make_async_copy(
                    pairs[2 * i + j], kv.at[side, pl.ds(begin, rows)], sems.at[2 * i + j]
                )
            )
        begin += rows
    for copy in copies:
        copy.start()
    for copy in copies:
        copy.wait()

    n_keys = kv.shape[1]
    chunk = 768 if n_keys % 768 == 0 else 576
    heads = q_ref.shape[1] // HEAD
    lane = lax.broadcasted_iota(jnp.int32, (q_ref.shape[0], HEAD), 1)
    kept = jnp.zeros(lane.shape, F32)
    for h in range(heads):
        lanes = slice(h * HEAD, (h + 1) * HEAD)
        query = q_ref[:, lanes]
        if first:
            peak = jnp.full((query.shape[0], 1), -jnp.inf, F32)
            total = jnp.zeros((query.shape[0], 1), F32)
            mixed = jnp.zeros((query.shape[0], HEAD), F32)
        else:
            peak, total = carried[0][:, h : h + 1], carried[0][:, heads + h : heads + h + 1]
            mixed = carried[1][:, lanes]
        for begin in range(0, n_keys, chunk):
            span = slice(begin, begin + chunk)
            scores = (
                lax.dot_general(
                    query,
                    kv[0, span, lanes],
                    (((1,), (1,)), ((), ())),
                    preferred_element_type=F32,
                )
                * SCORE_SCALE
            )
            new_peak = jnp.maximum(peak, jnp.max(scores, axis=1, keepdims=True))
            factor = jnp.exp2(peak - new_peak)
            probs = jnp.exp2(scores - new_peak)
            total = total * factor + jnp.sum(probs, axis=1, keepdims=True)
            mixed = mixed * factor + jnp.dot(
                probs.astype(BF16), kv[1, span, lanes], preferred_element_type=F32
            )
            peak = new_peak
        if last:
            outs[0][:, lanes] = (mixed / total).astype(BF16)
        else:
            kept = jnp.where(lane == h, peak, jnp.where(lane == heads + h, total, kept))
            outs[1][:, lanes] = mixed
    if not last:
        outs[0][...] = kept


def attend(core, query, pairs, carried, last):
    rows, width = query.shape
    heads = width // HEAD
    n_keys = sum(mine.shape[0] for mine, _ in pairs)
    state = [
        jax.ShapeDtypeStruct((rows, HEAD), F32),
        jax.ShapeDtypeStruct((rows, width), F32),
    ]
    in_vmem = pl.BlockSpec(memory_space=pltpu.VMEM)
    flat = [array for pair in pairs for array in pair]
    kernel = lambda *refs: attend_kernel(len(pairs), carried is None, last, *refs)
    return pl.pallas_call(
        kernel,
        out_shape=jax.ShapeDtypeStruct((rows, width), BF16) if last else state,
        grid_spec=pltpu.PrefetchScalarGridSpec(
            num_scalar_prefetch=1,
            grid=(1,),
            in_specs=[in_vmem]
            + [pl.BlockSpec(memory_space=pl.ANY)] * len(flat)
            + ([in_vmem] * 2 if carried is not None else []),
            out_specs=in_vmem if last else [in_vmem] * 2,
            scratch_shapes=[
                pltpu.VMEM((2, n_keys, width), BF16),
                pltpu.SemaphoreType.DMA((len(flat),)),
            ],
        ),
        compiler_params=pltpu.CompilerParams(vmem_limit_bytes=VMEM_BYTES),
        cost_estimate=pl.CostEstimate(
            flops=4 * rows * width * n_keys,
            bytes_accessed=4 * n_keys * width,
            transcendentals=rows * heads * n_keys,
        ),
        name="attend",
    )(core, query, *flat, *(carried if carried is not None else []))


def reorder_kernel(places, mine, other, out, sems):
    copies = []
    for source in (mine, other):
        for begin in range(0, source.shape[0], 192):
            i = len(copies)
            place = pl.multiple_of(places[i] * 192, 192)
            ends = (source.at[pl.ds(begin, 192)], out.at[pl.ds(place, 192)])
            copies.append(pltpu.make_async_copy(*ends, sems.at[i]))
    for copy in copies:
        copy.start()
    for copy in copies:
        copy.wait()


def reorder(mine, other, places):
    return pl.pallas_call(
        reorder_kernel,
        out_shape=jax.ShapeDtypeStruct((3072, 768), BF16),
        grid_spec=pltpu.PrefetchScalarGridSpec(
            num_scalar_prefetch=1,
            grid=(1,),
            in_specs=[pl.BlockSpec(memory_space=pl.ANY)] * 2,
            out_specs=pl.BlockSpec(memory_space=pltpu.VMEM),
            scratch_shapes=[pltpu.SemaphoreType.DMA((16,))],
        ),
        compiler_params=pltpu.CompilerParams(vmem_limit_bytes=8 * 2**20),
        cost_estimate=pl.CostEstimate(flops=0, bytes_accessed=4 * 3072 * 768, transcendentals=0),
        name="reorder",
    )(jnp.stack(places).astype(jnp.int32), mine, other)


def spread_out(w_out, core, c):
    def source(b, y, z, l, x):
        ctx, fsdp = y * 4 + z, l * 4 + x
        from_ctx, from_fsdp = 2 * fsdp + ((ctx % 2) ^ b), ctx // 2
        return (b, from_ctx // 4, from_ctx % 4, from_fsdp // 4, from_fsdp % 4)

    upper = (c % 2) != core
    return fetch(jnp.where(upper, w_out[192:], w_out[:192]), source)


def pack(wide):
    squares = wide[:, 64:65] + wide[:, 65:66]
    high = squares.astype(BF16).astype(F32)
    lane = lax.broadcasted_iota(jnp.int32, wide.shape, 1)
    return jnp.where(lane == 64, high, jnp.where(lane == 65, squares - high, wide)).astype(BF16)


def finish_kernel(n_groups, places, *refs):
    groups, refs = refs[:n_groups], refs[n_groups:]
    rows_ref, stream_ref, gain_ref, final_ref, wide_ref, packed_ref, mixed, sems = refs
    copies = []
    for i, group in enumerate(groups):
        place = mixed.at[:, pl.ds(pl.multiple_of(places[i] * 384, 128), 384)]
        copies.append(pltpu.make_async_copy(group, place, sems.at[i]))
    for copy in copies:
        copy.start()
    for copy in copies:
        copy.wait()
    term = jnp.dot(mixed[...], rows_ref[...], preferred_element_type=F32)
    state = (stream_ref[...].astype(F32) + term).astype(BF16).astype(F32)
    squares = jnp.sum(state * state, axis=1, keepdims=True)
    part = jnp.dot(
        state * gain_ref[...],
        final_ref[...],
        precision=lax.Precision.HIGHEST,
        preferred_element_type=F32,
    )
    lane = lax.broadcasted_iota(jnp.int32, part.shape, 1)
    wide = jnp.where(lane == 64, squares, part)
    wide_ref[...] = wide
    packed_ref[...] = pack(wide)


def finish(places, groups, rows, stream, gain, final):
    tokens, depth = stream.shape[0], rows.shape[0]
    in_vmem = pl.BlockSpec(memory_space=pltpu.VMEM)
    return pl.pallas_call(
        lambda *refs: finish_kernel(len(groups), *refs),
        out_shape=[jax.ShapeDtypeStruct((tokens, 128), dtype) for dtype in (F32, BF16)],
        grid_spec=pltpu.PrefetchScalarGridSpec(
            num_scalar_prefetch=1,
            grid=(1,),
            in_specs=[pl.BlockSpec(memory_space=pl.ANY)] * len(groups) + [in_vmem] * 4,
            out_specs=[in_vmem] * 2,
            scratch_shapes=[
                pltpu.VMEM((tokens, depth), BF16),
                pltpu.SemaphoreType.DMA((depth // 384,)),
            ],
        ),
        compiler_params=pltpu.CompilerParams(vmem_limit_bytes=VMEM_BYTES),
        cost_estimate=pl.CostEstimate(
            flops=2 * tokens * depth * rows.shape[1],
            bytes_accessed=2 * depth * (tokens + rows.shape[1]),
            transcendentals=0,
        ),
        name="finish",
    )(places.astype(jnp.int32), *groups, rows, stream, gain, final)


def plan(timestep):
    step_index = jnp.arange(STEPS, dtype=jnp.int32)
    betas = 0.0001 + (0.02 - 0.0001) * step_index.astype(jnp.float32) / (STEPS - 1)
    log_keep = jnp.cumsum(jnp.log1p(-betas))
    picked = (step_index == timestep[0]).astype(jnp.float32)
    beta_t = jnp.sum(picked * betas)
    abar_t = jnp.exp(jnp.sum(picked * log_keep))
    return (beta_t, abar_t)


def body(
    hidden, stream, w_query, w_key, w_value, w_out, out_gain, w_final, latents, noise, timestep
):
    inputs = hidden[0]
    core, c, f = (lax.axis_index(name) for name in AXES)
    y, z, l, x = c // 4, c % 4, f // 4, f % 4
    core_id = core.reshape(1).astype(jnp.int32)

    def at(dy, dz):
        return ((y + dy) % 4) * 4 + (z + dz) % 4

    weight = jnp.where(core == 0, w_key, w_value)
    z1, z3 = from_z(weight, 1), from_z(weight, -1)
    y1, y3 = from_y(weight, 1), from_y(weight, -1)
    query_near = fetch(w_query, near_of("y"))
    z1, z3, y1, y3, query_near, weight, inputs, w_query, w_out = together(
        z1, z3, y1, y3, query_near, weight, inputs, w_query, w_out
    )

    z2, y2 = from_z(weight, 2), from_y(weight, 2)
    query_far = fetch(w_query, far_of("y"))
    given = fetch(inputs, lambda b, *at: (0, *at) if b else None)
    z2, y2, query_far, given = together(z2, y2, query_far, given)

    others = join([z1, z3, z2])
    query_block = pair_of(core, w_query, query_near, query_far)
    others, query_block, given, w_out = together(others, query_block, given, w_out)
    ahead, behind = from_y(others, 1), from_y(others, -1)
    query_ahead, query_behind = from_z(query_block, 1), from_z(query_block, -1)
    spread = spread_out(w_out, core, c)
    source = jnp.where(core == 0, inputs, given)
    order = [at(0, 0), at(1, 0), at(3, 0), at(2, 0), at(0, 1), at(0, 3), at(0, 2)]
    total = project(source, [weight, y1, y3, y2, others], order, None, F32)
    ahead, behind, total = together(ahead, behind, total)

    half = others.shape[0] // 2
    far_top, far_bottom = from_y(ahead[:half], 1), from_y(behind[half:], -1)
    order = [at(dy, dz) for dy in (1, 3) for dz in (1, 3, 2)]
    total = project(source, [ahead, behind], order, total, F32)
    total, query_ahead, query_behind = together(total, query_ahead, query_behind)
    half = query_block.shape[0] // 2
    query_top = from_z(query_ahead[:half], 1)
    query_bottom = from_z(query_behind[half:], -1)
    far_top, far_bottom, total, spread = together(far_top, far_bottom, total, spread)
    order = [at(2, dz) for dz in (1, 3, 2)]
    kv = project(source, [far_top, far_bottom], order, total, BF16)

    z1, z3, y1 = from_z(kv, 1), from_z(kv, -1), from_y(kv, 1)
    z1, z3, y1, kv, query_top, query_bottom = together(z1, z3, y1, kv, query_top, query_bottom)

    z2, y3, y2 = from_z(kv, 2), from_y(kv, -1), from_y(kv, 2)
    kv_swapped = swap_cores(kv)
    mine = join([query_block, query_ahead, query_behind, query_top, query_bottom])
    mine_swapped = swap_cores(mine)
    order = pair_order(y, z, l, core, "y", (0, 1, 3, 2))
    query = project(inputs, [mine], order, None, F32)
    spread_swapped = swap_cores(spread)
    spread = jnp.where(
        c % 2 == core,
        jnp.concatenate([spread, spread_swapped], axis=1),
        jnp.concatenate([spread_swapped, spread], axis=1),
    )
    beta_t, abar_t = plan(timestep)
    gain, final = out_gain[None], jnp.pad(w_final, ((0, 0), (0, 64)))
    z2, y3, y2, kv_swapped, mine_swapped, query, spread, beta_t, abar_t, gain, final = together(
        z2, y3, y2, kv_swapped, mine_swapped, query, spread, beta_t, abar_t, gain, final
    )

    others = join([z1, z3, z2])
    others, mine_swapped, spread, y1, y2, y3 = together(others, mine_swapped, spread, y1, y2, y3)
    ahead, behind = from_y(others, 1), from_y(others, -1)
    others_swapped = swap_cores(others)
    out_near, out_far = fetch(spread, near_of("z")), fetch(spread, far_of("z"))
    order = pair_order(y, z, l, 1 - core, "y", (0, 1, 3, 2))
    query = project(inputs, [mine_swapped], order, query, BF16)
    near = join([y1, y3, y2])
    carried = attend(core_id, query, [(kv, kv_swapped), (others, others_swapped)], None, False)
    ahead, behind, near, out_near, out_far, *carried = together(
        ahead, behind, near, out_near, out_far, *carried
    )

    half = others.shape[0] // 2
    far_top, far_bottom = from_y(ahead[:half], 1), from_y(behind[half:], -1)
    near_swapped, ahead_swapped, behind_swapped = (swap_cores(part) for part in (near, ahead, behind))
    out_block = pair_of(core, spread, out_near, out_far)
    carried = attend(core_id, query, [(near, near_swapped)], carried, False)
    out_block, *carried = together(out_block, *carried)
    out_ahead, out_behind = from_y(out_block, 1), from_y(out_block, -1)
    pairs = [(ahead, ahead_swapped), (behind, behind_swapped)]
    carried = attend(core_id, query, pairs, carried, False)
    far_top, far_bottom, *carried = together(far_top, far_bottom, *carried)

    top_swapped, bottom_swapped = swap_cores(far_top), swap_cores(far_bottom)
    pairs = [(far_top, top_swapped), (far_bottom, bottom_swapped)]
    mixed = attend(core_id, query, pairs, carried, True)
    mixed, out_ahead, out_behind, out_block = together(mixed, out_ahead, out_behind, out_block)

    mixed_l = fetch(mixed, along("l", 1))
    mixed_x = [fetch(mixed, along("x", step)) for step in (1, 3, 2)]
    out_two = from_y(out_block, 2)
    mixed_l, out_two, mixed, *mixed_x = together(mixed_l, out_two, mixed, *mixed_x)
    mine = join([out_block, out_ahead, out_behind, out_two])
    groups = [mixed, mixed_l, *mixed_x]
    groups += [fetch(mixed_l, along("x", step)) for step in (1, 3, 2)]
    steps = [(0, 0), (1, 0), (0, 1), (0, 3), (0, 2), (1, 1), (1, 3), (1, 2)]
    places = [(l + dl) % 2 * 4 + (x + dx) % 4 for dl, dx in steps]
    rows_from = [
        place for side in (core, 1 - core) for place in pair_order(y, z, l, side, "z", (0, 1, 3, 2))
    ]
    out_rows = reorder(mine, swap_cores(mine), rows_from)
    wide, packed = finish(jnp.stack(places), groups, out_rows, stream[0], gain, final)

    wide += fetch(packed, along("l", 1)).astype(F32)
    packed = pack(wide)
    wide += sum(fetch(packed, along("x", step)).astype(F32) for step in (1, 2, 3))
    square_total = wide[:, 64:65] + wide[:, 65:66]
    eps_branch = wide[:, :64] * lax.rsqrt(square_total / D + 1e-06)
    moved = (latents[0] - beta_t / jnp.sqrt(1.0 - abar_t) * eps_branch) / jnp.sqrt(1.0 - beta_t)
    stepped = moved + jnp.sqrt(beta_t) * noise[0]
    return (eps_branch[None], stepped[None])


def solution(mesh):
    return jax.shard_map(
        body,
        mesh=mesh,
        in_specs=(
            P("branch", "ctx", None),
            P("branch", "ctx", "fsdp"),
            P("ctx", "fsdp"),
            P("ctx", "fsdp"),
            P("ctx", "fsdp"),
            P("fsdp", "ctx"),
            P("fsdp"),
            P("fsdp", None),
            P("branch", "ctx", None),
            P("branch", "ctx", None),
            P(),
        ),
        out_specs=(P("branch", "ctx", None), P("branch", "ctx", None)),
        check_vma=False,
    )
```

```python
import math

import jax
import jax.numpy as jnp
from jax import lax
from jax.experimental import pallas as pl
from jax.experimental.pallas import tpu as pltpu
from jax.sharding import PartitionSpec as P

D = 6144
HEAD = 128
STEPS = 1000
AXES = ("branch", "ctx", "fsdp")
SCORE_SCALE = HEAD ** (-0.5) * math.log2(math.e)
VMEM_BYTES = 16 * 2**20
F32 = jnp.float32
BF16 = jnp.bfloat16


def line(b, y, z, l, x):
    return b * 128 + ((y % 4) * 4 + z % 4) * 8 + (l % 2) * 4 + x % 4


def fetch(value, source):
    route = []
    for b in range(2):
        for y in range(4):
            for z in range(4):
                for l in range(2):
                    for x in range(4):
                        found = source(b, y, z, l, x)
                        if found is not None:
                            route.append((line(*found), line(b, y, z, l, x)))
    return lax.ppermute(value, AXES, route)


def along(axis, step):
    def source(*device):
        moved = list(device)
        moved["byzlx".index(axis)] += step
        return moved

    return source


def swap_cores(value):
    return fetch(value, lambda b, y, z, l, x: (1 - b, y, z, l, x))


def together(*values):
    return lax.optimization_barrier(values)


def from_y(value, step):
    return fetch(value, along("y", step))


def from_z(value, step):
    return fetch(value, along("z", step))


def join_kernel(*refs):
    sources, out, sems = refs[:-2], refs[-2], refs[-1]
    copies, begin = [], 0
    for i, source in enumerate(sources):
        rows = source.shape[0]
        copies.append(pltpu.make_async_copy(source, out.at[pl.ds(begin, rows)], sems.at[i]))
        begin += rows
    for copy in copies:
        copy.start()
    for copy in copies:
        copy.wait()


def join(arrays):
    shape = (sum(array.shape[0] for array in arrays), arrays[0].shape[1])
    return pl.pallas_call(
        join_kernel,
        out_shape=jax.ShapeDtypeStruct(shape, arrays[0].dtype),
        in_specs=[pl.BlockSpec(memory_space=pl.ANY)] * len(arrays),
        out_specs=pl.BlockSpec(memory_space=pltpu.VMEM),
        scratch_shapes=[pltpu.SemaphoreType.DMA((len(arrays),))],
        compiler_params=pltpu.CompilerParams(vmem_limit_bytes=8 * 2**20),
        cost_estimate=pl.CostEstimate(
            flops=0, bytes_accessed=4 * shape[0] * shape[1], transcendentals=0
        ),
        name="join",
    )(*arrays)


def near_of(axis):
    def source(*device):
        device = list(device)
        step = 1 - 2 * device[3]
        device["byzlx".index(axis)] += step if device[0] == 0 else -step
        return device

    return source


def far_of(axis):
    return lambda *device: along(axis, 2)(*device) if device[0] == 1 else None


def pair_of(core, piece, near, far):
    return jnp.where(
        core == 0, jnp.concatenate([piece, near], axis=0), jnp.concatenate([near, far], axis=0)
    )


def pair_order(y, z, l, core, axis, steps):
    sign = 1 - 2 * l
    low = jnp.where(core == 0, 0, -sign)
    high = jnp.where(core == 0, sign, 2)
    places = [(step, near) for step in steps for near in (low, high)]
    if axis == "y":
        return [((y + near + 4) % 4) * 4 + (z + step) % 4 for step, near in places]
    return [((y + step) % 4) * 4 + (z + near + 4) % 4 for step, near in places]


def project_kernel(n_weights, order, x_ref, *refs):
    weights, refs = refs[:n_weights], refs[n_weights:]
    totals, (out_ref, x_all, w_all, acc, sems) = refs[:-5], refs[-5:]
    copies = []
    for i in range(w_all.shape[0] // 384):
        place = pl.multiple_of(order[i] * 384, 128)
        copies.append((x_ref.at[:, pl.ds(place, 384)], x_all.at[:, pl.ds(i * 384, 384)]))
    begin = 0
    for weight in weights:
        copies.append((weight, w_all.at[pl.ds(begin, weight.shape[0])]))
        begin += weight.shape[0]
    copies = [pltpu.make_async_copy(*ends, sems.at[i]) for i, ends in enumerate(copies)]
    for copy in copies:
        copy.start()
    for copy in copies:
        copy.wait()
    depth = w_all.shape[0]
    step = next(size for size in (768, 1152, 384) if depth % size == 0)
    acc[...] = totals[0][...] if totals else jnp.zeros_like(acc)

    def add(i, _):
        span = pl.ds(pl.multiple_of(i * step, step), step)
        acc[...] += jnp.dot(x_all[:, span], w_all[span, :], preferred_element_type=F32)

    lax.fori_loop(0, depth // step, add, None)
    out_ref[...] = acc[...].astype(out_ref.dtype)


def project(x, weights, order, total, dtype):
    rows, cols = x.shape[0], weights[0].shape[1]
    depth = sum(weight.shape[0] for weight in weights)
    in_vmem, anywhere = (pl.BlockSpec(memory_space=space) for space in (pltpu.VMEM, pl.ANY))
    return pl.pallas_call(
        lambda *refs: project_kernel(len(weights), *refs),
        out_shape=jax.ShapeDtypeStruct((rows, cols), dtype),
        grid_spec=pltpu.PrefetchScalarGridSpec(
            num_scalar_prefetch=1,
            grid=(1,),
            in_specs=[anywhere] * (1 + len(weights)) + [in_vmem] * (total is not None),
            out_specs=in_vmem,
            scratch_shapes=[
                pltpu.VMEM((rows, depth), BF16),
                pltpu.VMEM((depth, cols), BF16),
                pltpu.VMEM((rows, cols), F32),
                pltpu.SemaphoreType.DMA((depth // 384 + len(weights),)),
            ],
        ),
        compiler_params=pltpu.CompilerParams(vmem_limit_bytes=VMEM_BYTES),
        cost_estimate=pl.CostEstimate(
            flops=2 * rows * cols * depth,
            bytes_accessed=2 * (rows + cols) * depth + 8 * rows * cols,
            transcendentals=0,
        ),
        name="project",
    )(jnp.stack(list(order)).astype(jnp.int32), x, *weights, *([total] if total is not None else []))


def attend_kernel(n_pairs, first, last, core, q_ref, *refs):
    pairs, refs = refs[: 2 * n_pairs], refs[2 * n_pairs :]
    if not first:
        carried, refs = refs[:2], refs[2:]
    outs, refs = (refs[:1], refs[1:]) if last else (refs[:2], refs[2:])
    kv, sems = refs
    copies, begin = [], 0
    for i in range(n_pairs):
        rows = pairs[2 * i].shape[0]
        for j, side in enumerate((core[0], 1 - core[0])):
            copies.append(
                pltpu.make_async_copy(
                    pairs[2 * i + j], kv.at[side, pl.ds(begin, rows)], sems.at[2 * i + j]
                )
            )
        begin += rows
    for copy in copies:
        copy.start()
    for copy in copies:
        copy.wait()

    n_keys = kv.shape[1]
    chunk = 768 if n_keys % 768 == 0 else n_keys
    heads = q_ref.shape[1] // HEAD
    lane = lax.broadcasted_iota(jnp.int32, (q_ref.shape[0], HEAD), 1)

    def one_head(h, kept):
        lanes = pl.ds(pl.multiple_of(h * HEAD, HEAD), HEAD)
        query = q_ref[:, lanes]
        if first:
            peak = jnp.full((query.shape[0], 1), -jnp.inf, F32)
            total = jnp.zeros((query.shape[0], 1), F32)
            mixed = jnp.zeros((query.shape[0], HEAD), F32)
        else:
            kept_in = carried[0][...]
            peak = jnp.max(jnp.where(lane == h, kept_in, -jnp.inf), axis=1, keepdims=True)
            total = jnp.sum(jnp.where(lane == heads + h, kept_in, 0.0), axis=1, keepdims=True)
            mixed = carried[1][:, lanes]
        for begin in range(0, n_keys, chunk):
            span = pl.ds(begin, chunk)
            scores = (
                lax.dot_general(
                    query,
                    kv[0, span, lanes],
                    (((1,), (1,)), ((), ())),
                    preferred_element_type=F32,
                )
                * SCORE_SCALE
            )
            new_peak = jnp.maximum(peak, jnp.max(scores, axis=1, keepdims=True))
            factor = jnp.exp2(peak - new_peak)
            probs = jnp.exp2(scores - new_peak)
            widened = jnp.concatenate([kv[1, span, lanes], jnp.ones((chunk, HEAD), BF16)], axis=1)
            added = jnp.dot(probs.astype(BF16), widened, preferred_element_type=F32)
            total = total * factor + added[:, HEAD : HEAD + 1]
            mixed = mixed * factor + added[:, :HEAD]
            peak = new_peak
        if last:
            outs[0][:, lanes] = (mixed / total).astype(BF16)
            return kept
        outs[1][:, lanes] = mixed
        return jnp.where(lane == h, peak, jnp.where(lane == heads + h, total, kept))

    kept = lax.fori_loop(0, heads, one_head, jnp.zeros(lane.shape, F32), unroll=last)
    if not last:
        outs[0][...] = kept


def attend(core, query, pairs, carried, last):
    rows, width = query.shape
    heads = width // HEAD
    n_keys = sum(mine.shape[0] for mine, _ in pairs)
    state = [
        jax.ShapeDtypeStruct((rows, HEAD), F32),
        jax.ShapeDtypeStruct((rows, width), F32),
    ]
    in_vmem = pl.BlockSpec(memory_space=pltpu.VMEM)
    flat = [array for pair in pairs for array in pair]
    kernel = lambda *refs: attend_kernel(len(pairs), carried is None, last, *refs)
    return pl.pallas_call(
        kernel,
        out_shape=jax.ShapeDtypeStruct((rows, width), BF16) if last else state,
        grid_spec=pltpu.PrefetchScalarGridSpec(
            num_scalar_prefetch=1,
            grid=(1,),
            in_specs=[in_vmem]
            + [pl.BlockSpec(memory_space=pl.ANY)] * len(flat)
            + ([in_vmem] * 2 if carried is not None else []),
            out_specs=in_vmem if last else [in_vmem] * 2,
            scratch_shapes=[
                pltpu.VMEM((2, n_keys, width), BF16),
                pltpu.SemaphoreType.DMA((len(flat),)),
            ],
        ),
        compiler_params=pltpu.CompilerParams(vmem_limit_bytes=VMEM_BYTES),
        cost_estimate=pl.CostEstimate(
            flops=4 * rows * width * n_keys,
            bytes_accessed=4 * n_keys * width,
            transcendentals=rows * heads * n_keys,
        ),
        name="attend",
    )(core, query, *flat, *(carried if carried is not None else []))


def reorder_kernel(places, mine, other, out, sems):
    copies = []
    for source in (mine, other):
        for begin in range(0, source.shape[0], 192):
            i = len(copies)
            place = pl.multiple_of(places[i] * 192, 192)
            ends = (source.at[pl.ds(begin, 192)], out.at[pl.ds(place, 192)])
            copies.append(pltpu.make_async_copy(*ends, sems.at[i]))
    for copy in copies:
        copy.start()
    for copy in copies:
        copy.wait()


def reorder(mine, other, places):
    return pl.pallas_call(
        reorder_kernel,
        out_shape=jax.ShapeDtypeStruct((3072, 768), BF16),
        grid_spec=pltpu.PrefetchScalarGridSpec(
            num_scalar_prefetch=1,
            grid=(1,),
            in_specs=[pl.BlockSpec(memory_space=pl.ANY)] * 2,
            out_specs=pl.BlockSpec(memory_space=pltpu.VMEM),
            scratch_shapes=[pltpu.SemaphoreType.DMA((16,))],
        ),
        compiler_params=pltpu.CompilerParams(vmem_limit_bytes=8 * 2**20),
        cost_estimate=pl.CostEstimate(flops=0, bytes_accessed=4 * 3072 * 768, transcendentals=0),
        name="reorder",
    )(jnp.stack(places).astype(jnp.int32), mine, other)


def spread_out(w_out, core, c):
    def source(b, y, z, l, x):
        ctx, fsdp = y * 4 + z, l * 4 + x
        from_ctx, from_fsdp = 2 * fsdp + ((ctx % 2) ^ b), ctx // 2
        return (b, from_ctx // 4, from_ctx % 4, from_fsdp // 4, from_fsdp % 4)

    upper = (c % 2) != core
    return fetch(jnp.where(upper, w_out[192:], w_out[:192]), source)


def pack(wide):
    squares = wide[:, 64:65] + wide[:, 65:66]
    high = squares.astype(BF16).astype(F32)
    lane = lax.broadcasted_iota(jnp.int32, wide.shape, 1)
    return jnp.where(lane == 64, high, jnp.where(lane == 65, squares - high, wide)).astype(BF16)


def finish_kernel(n_groups, places, *refs):
    groups, refs = refs[:n_groups], refs[n_groups:]
    rows_ref, stream_ref, gain_ref, final_ref, wide_ref, packed_ref, mixed, acc, sems = refs
    copies = []
    for i, group in enumerate(groups):
        place = mixed.at[:, pl.ds(pl.multiple_of(places[i] * 384, 128), 384)]
        copies.append(pltpu.make_async_copy(group, place, sems.at[i]))
    for copy in copies:
        copy.start()
    for copy in copies:
        copy.wait()
    acc[...] = stream_ref[...].astype(F32)

    def add(i, _):
        span = pl.ds(pl.multiple_of(i * 768, 768), 768)
        acc[...] += jnp.dot(mixed[:, span], rows_ref[span, :], preferred_element_type=F32)

    lax.fori_loop(0, mixed.shape[1] // 768, add, None)
    state = acc[...].astype(BF16).astype(F32)
    squares = jnp.sum(state * state, axis=1, keepdims=True)
    part = jnp.dot(
        state * gain_ref[...],
        final_ref[...],
        precision=lax.Precision.HIGHEST,
        preferred_element_type=F32,
    )
    lane = lax.broadcasted_iota(jnp.int32, part.shape, 1)
    wide = jnp.where(lane == 64, squares, part)
    wide_ref[...] = wide
    packed_ref[...] = pack(wide)


def finish(places, groups, rows, stream, gain, final):
    tokens, depth = stream.shape[0], rows.shape[0]
    in_vmem = pl.BlockSpec(memory_space=pltpu.VMEM)
    return pl.pallas_call(
        lambda *refs: finish_kernel(len(groups), *refs),
        out_shape=[jax.ShapeDtypeStruct((tokens, 128), dtype) for dtype in (F32, BF16)],
        grid_spec=pltpu.PrefetchScalarGridSpec(
            num_scalar_prefetch=1,
            grid=(1,),
            in_specs=[pl.BlockSpec(memory_space=pl.ANY)] * len(groups) + [in_vmem] * 4,
            out_specs=[in_vmem] * 2,
            scratch_shapes=[
                pltpu.VMEM((tokens, depth), BF16),
                pltpu.VMEM((tokens, rows.shape[1]), F32),
                pltpu.SemaphoreType.DMA((depth // 384,)),
            ],
        ),
        compiler_params=pltpu.CompilerParams(vmem_limit_bytes=VMEM_BYTES),
        cost_estimate=pl.CostEstimate(
            flops=2 * tokens * depth * rows.shape[1],
            bytes_accessed=2 * depth * (tokens + rows.shape[1]),
            transcendentals=0,
        ),
        name="finish",
    )(places.astype(jnp.int32), *groups, rows, stream, gain, final)


def plan(timestep):
    step_index = jnp.arange(STEPS, dtype=jnp.int32)
    betas = 0.0001 + (0.02 - 0.0001) * step_index.astype(jnp.float32) / (STEPS - 1)
    log_keep = jnp.cumsum(jnp.log1p(-betas))
    picked = (step_index == timestep[0]).astype(jnp.float32)
    beta_t = jnp.sum(picked * betas)
    abar_t = jnp.exp(jnp.sum(picked * log_keep))
    return (beta_t, abar_t)


def body(
    hidden, stream, w_query, w_key, w_value, w_out, out_gain, w_final, latents, noise, timestep
):
    inputs = hidden[0]
    core, c, f = (lax.axis_index(name) for name in AXES)
    y, z, l, x = c // 4, c % 4, f // 4, f % 4
    core_id = core.reshape(1).astype(jnp.int32)

    def at(dy, dz):
        return ((y + dy) % 4) * 4 + (z + dz) % 4

    weight = jnp.where(core == 0, w_key, w_value)
    z1, z3 = from_z(weight, 1), from_z(weight, -1)
    y1, y3 = from_y(weight, 1), from_y(weight, -1)
    query_near = fetch(w_query, near_of("y"))
    z1, z3, y1, y3, query_near, weight, inputs, w_query, w_out = together(
        z1, z3, y1, y3, query_near, weight, inputs, w_query, w_out
    )

    z2, y2 = from_z(weight, 2), from_y(weight, 2)
    query_far = fetch(w_query, far_of("y"))
    given = fetch(inputs, lambda b, *at: (0, *at) if b else None)
    z2, y2, query_far, given = together(z2, y2, query_far, given)

    others = join([z1, z3, z2])
    query_block = pair_of(core, w_query, query_near, query_far)
    others, query_block, given, w_out = together(others, query_block, given, w_out)
    ahead, behind = from_y(others, 1), from_y(others, -1)
    query_ahead, query_behind = from_z(query_block, 1), from_z(query_block, -1)
    spread = spread_out(w_out, core, c)
    source = jnp.where(core == 0, inputs, given)
    order = [at(0, 0), at(1, 0), at(3, 0), at(2, 0), at(0, 1), at(0, 3), at(0, 2)]
    total = project(source, [weight, y1, y3, y2, others], order, None, F32)
    ahead, behind, total = together(ahead, behind, total)

    half = others.shape[0] // 2
    far_top, far_bottom = from_y(ahead[:half], 1), from_y(behind[half:], -1)
    order = [at(dy, dz) for dy in (1, 3) for dz in (1, 3, 2)]
    total = project(source, [ahead, behind], order, total, F32)
    total, query_ahead, query_behind = together(total, query_ahead, query_behind)
    half = query_block.shape[0] // 2
    query_top = from_z(query_ahead[:half], 1)
    query_bottom = from_z(query_behind[half:], -1)
    far_top, far_bottom, total, spread = together(far_top, far_bottom, total, spread)
    order = [at(2, dz) for dz in (1, 3, 2)]
    kv = project(source, [far_top, far_bottom], order, total, BF16)

    z1, z3, y1 = from_z(kv, 1), from_z(kv, -1), from_y(kv, 1)
    z1, z3, y1, kv, query_top, query_bottom = together(z1, z3, y1, kv, query_top, query_bottom)

    z2, y3, y2 = from_z(kv, 2), from_y(kv, -1), from_y(kv, 2)
    kv_swapped = swap_cores(kv)
    mine = join([query_block, query_ahead, query_behind, query_top, query_bottom])
    mine_swapped = swap_cores(mine)
    order = pair_order(y, z, l, core, "y", (0, 1, 3, 2))
    query = project(inputs, [mine], order, None, F32)
    spread_swapped = swap_cores(spread)
    spread = jnp.where(
        c % 2 == core,
        jnp.concatenate([spread, spread_swapped], axis=1),
        jnp.concatenate([spread_swapped, spread], axis=1),
    )
    beta_t, abar_t = plan(timestep)
    gain, final = out_gain[None], jnp.pad(w_final, ((0, 0), (0, 64)))
    z2, y3, y2, kv_swapped, mine_swapped, query, spread, beta_t, abar_t, gain, final = together(
        z2, y3, y2, kv_swapped, mine_swapped, query, spread, beta_t, abar_t, gain, final
    )

    others = join([z1, z3, z2])
    others, mine_swapped, spread, y1, y2, y3 = together(others, mine_swapped, spread, y1, y2, y3)
    ahead, behind = from_y(others, 1), from_y(others, -1)
    others_swapped = swap_cores(others)
    out_near, out_far = fetch(spread, near_of("z")), fetch(spread, far_of("z"))
    order = pair_order(y, z, l, 1 - core, "y", (0, 1, 3, 2))
    query = project(inputs, [mine_swapped], order, query, BF16)
    near = join([y1, y3, y2])
    carried = attend(core_id, query, [(kv, kv_swapped), (others, others_swapped)], None, False)
    ahead, behind, near, out_near, out_far, *carried = together(
        ahead, behind, near, out_near, out_far, *carried
    )

    half = others.shape[0] // 2
    far_top, far_bottom = from_y(ahead[:half], 1), from_y(behind[half:], -1)
    near_swapped, ahead_swapped, behind_swapped = (swap_cores(part) for part in (near, ahead, behind))
    out_block = pair_of(core, spread, out_near, out_far)
    carried = attend(core_id, query, [(near, near_swapped)], carried, False)
    out_block, *carried = together(out_block, *carried)
    out_ahead, out_behind = from_y(out_block, 1), from_y(out_block, -1)
    pairs = [(ahead, ahead_swapped), (behind, behind_swapped)]
    carried = attend(core_id, query, pairs, carried, False)
    far_top, far_bottom, *carried = together(far_top, far_bottom, *carried)

    top_swapped, bottom_swapped = swap_cores(far_top), swap_cores(far_bottom)
    pairs = [(far_top, top_swapped), (far_bottom, bottom_swapped)]
    mixed = attend(core_id, query, pairs, carried, True)
    mixed, out_ahead, out_behind, out_block = together(mixed, out_ahead, out_behind, out_block)

    mixed_l = fetch(mixed, along("l", 1))
    mixed_x = [fetch(mixed, along("x", step)) for step in (1, 3, 2)]
    out_two = from_y(out_block, 2)
    mixed_l, out_two, mixed, *mixed_x = together(mixed_l, out_two, mixed, *mixed_x)
    mine = join([out_block, out_ahead, out_behind, out_two])
    groups = [mixed, mixed_l, *mixed_x]
    groups += [fetch(mixed_l, along("x", step)) for step in (1, 3, 2)]
    steps = [(0, 0), (1, 0), (0, 1), (0, 3), (0, 2), (1, 1), (1, 3), (1, 2)]
    places = [(l + dl) % 2 * 4 + (x + dx) % 4 for dl, dx in steps]
    rows_from = [
        place for side in (core, 1 - core) for place in pair_order(y, z, l, side, "z", (0, 1, 3, 2))
    ]
    out_rows = reorder(mine, swap_cores(mine), rows_from)
    wide, packed = finish(jnp.stack(places), groups, out_rows, stream[0], gain, final)

    wide += fetch(packed, along("l", 1)).astype(F32)
    packed = pack(wide)
    wide += sum(fetch(packed, along("x", step)).astype(F32) for step in (1, 2, 3))
    square_total = wide[:, 64:65] + wide[:, 65:66]
    eps_branch = wide[:, :64] * lax.rsqrt(square_total / D + 1e-06)
    moved = (latents[0] - beta_t / jnp.sqrt(1.0 - abar_t) * eps_branch) / jnp.sqrt(1.0 - beta_t)
    stepped = moved + jnp.sqrt(beta_t) * noise[0]
    return (eps_branch[None], stepped[None])


def solution(mesh):
    return jax.shard_map(
        body,
        mesh=mesh,
        in_specs=(
            P("branch", "ctx", None),
            P("branch", "ctx", "fsdp"),
            P("ctx", "fsdp"),
            P("ctx", "fsdp"),
            P("ctx", "fsdp"),
            P("fsdp", "ctx"),
            P("fsdp"),
            P("fsdp", None),
            P("branch", "ctx", None),
            P("branch", "ctx", None),
            P(),
        ),
        out_specs=(P("branch", "ctx", None), P("branch", "ctx", None)),
        check_vma=False,
    )
```
